32 devices in a mesh: section: 2 (over x), seq: 4 (over y, core), tensor: 4 (over z).
Axes of the slice: x: 2, y: 2, z: 4, core: 2. Of those that a mesh axis runs over, the one named last changes fastest.
Arguments:
- tokens: bfloat16 [2, 2048, 1024], P(None, ('seq', 'tensor')), may hold values from -6 to 6
- w_qkv: bfloat16 [2, 1024, 3, 1024], P('section', None, None, 'tensor'), may hold values from -0.1875 to 0.1875
- w_out: bfloat16 [2, 1024, 1024], P('section', 'tensor'), may hold values from -0.25 to 0.25
- w_gate_up: bfloat16 [2, 1024, 2, 2816], P('section', None, None, 'tensor'), may hold values from -0.1875 to 0.1875
- w_down: bfloat16 [2, 2816, 1024], P('section', 'tensor'), may hold values from -0.109375 to 0.109375
- norm_gains: float32 [2, 2, 1024], P('section'), may hold values from 0.5 to 1.5
- log_decay: float32 [2, 2048, 16], P(None, 'seq', 'tensor'), may hold values from -2 to 0
- segment_ids: int32 [2, 2048], P(None, 'seq'), may hold values from 0 to 4, as said below
- cotangent: bfloat16 [2, 2048, 1024], P(None, ('seq', 'tensor')), may hold values from -6 to 6
Outputs:
- layer_outputs: bfloat16 [2, 2, 2048, 1024], P('section', None, ('seq', 'tensor'))
- input_grads: float32 [2, 2, 2048, 1024], P('section', None, ('seq', 'tensor'))
- grad_qkv: float32 [2, 1024, 3, 1024], P('section', None, None, 'tensor')
- grad_out: float32 [2, 1024, 1024], P('section', 'tensor')
- grad_gate_up: float32 [2, 1024, 2, 2816], P('section', None, None, 'tensor')
- grad_down: float32 [2, 2816, 1024], P('section', 'tensor')
- grad_gains: float32 [2, 2, 1024], P('section')
The draws below stay inside these ranges and needn't reach their ends.
Inputs may be any that keep to these rules, and one draw needn't show every extreme that they name: `segment_ids`: within a stream the ids never fall and number the documents from 0. One stream, drawn from the seed, holds five documents, and the one with id 2 starts within the first 512 tokens and ends within the last 512. In the other, a document ends near every multiple of 2048 tokens before the stream's end, within 512 of it on either side.
All inputs are finite; a program needn't handle non-finite values.
Results may differ from the reference program's by a relative error of at most 0.03.
Values may be sent and summed in bfloat16 or wider, within the bound.
No kernel may reach another device: no remote copies, remote signals or barrier semaphores. Data moves between devices by JAX's collectives and lax.ppermute only.
A program may use at most 192 MiB of HBM per device.

```python
import math
import jax
import jax.numpy as jnp
from jax import lax

D = 1024
HEADS = 16
HDIM = 64
FF = 2816
BLOCK = 64
MICRO = 2
TOK_MB = 512
SEQ_LEN = 2048


def draw_log_decay(key, part):
    key = jax.random.fold_in(key, 11)
    streams = jax.random.split(key, 7)
    fast_share = 0.5
    slow_top = 0.3
    fast = jax.random.uniform(streams[0], (MICRO, 1, HEADS)) < fast_share
    fast_rate = jnp.exp(jax.random.uniform(streams[1], (MICRO, 1, HEADS), minval=math.log(1.0 / 50.0), maxval=math.log(1.0 / 30.0)))
    slow_rate = jnp.exp(jax.random.uniform(streams[2], (MICRO, 1, HEADS), minval=math.log(0.1), maxval=math.log(slow_top))) / SEQ_LEN
    reference_level = jnp.where(fast, fast_rate, slow_rate)
    ranges = SEQ_LEN // TOK_MB
    processor_multiplier = jnp.exp(jax.random.uniform(streams[3], (MICRO, ranges, 1, HEADS), minval=math.log(0.5), maxval=math.log(2.0)))
    processor_multiplier = jnp.broadcast_to(processor_multiplier, (MICRO, ranges, TOK_MB, HEADS)).reshape(MICRO, SEQ_LEN, HEADS)
    jaggedness = jax.random.uniform(streams[4], (MICRO, SEQ_LEN, HEADS), minval=0.6, maxval=1.4)
    spots = jax.random.randint(streams[5], (MICRO, 1, 3), 0, SEQ_LEN)
    loss_values = jnp.log(1.0 - jax.random.uniform(streams[6], (MICRO, 3, HEADS), minval=0.2, maxval=0.35))
    places = jnp.arange(SEQ_LEN, dtype=jnp.int32)[None, :, None]
    removed_entries = (places == spots).astype(jnp.float32)
    spike_events = jnp.sum(removed_entries[:, :, :, None] * loss_values[:, None, :, :], axis=2)
    return (spike_events - reference_level * processor_multiplier * jaggedness).astype(jnp.float32)


def draw_segment_ids(key, part):
    key = jax.random.fold_in(key, 23)
    streams = jax.random.split(key, 6)
    halfway = TOK_MB // 2
    first_cut = jax.random.randint(streams[0], (MICRO, 1), 1, halfway)
    second_cut = jax.random.randint(streams[1], (MICRO, 1), halfway, TOK_MB)
    third_cut = jax.random.randint(streams[2], (MICRO, 1), SEQ_LEN - TOK_MB, SEQ_LEN - halfway)
    fourth_cut = jax.random.randint(streams[3], (MICRO, 1), SEQ_LEN - halfway, SEQ_LEN)
    places = jnp.arange(SEQ_LEN, dtype=jnp.int32)[None, :]
    spanning = (places >= first_cut).astype(jnp.int32) + (places >= second_cut).astype(jnp.int32)
    spanning = spanning + (places >= third_cut).astype(jnp.int32) + (places >= fourth_cut).astype(jnp.int32)
    cut_count = SEQ_LEN // (4 * TOK_MB) - 1
    chopped = jnp.zeros((1, SEQ_LEN), jnp.int32)
    if cut_count > 0:
        jitter = jax.random.randint(streams[4], (1, cut_count), -TOK_MB, TOK_MB)
        cuts = (jnp.arange(1, cut_count + 1, dtype=jnp.int32) * (4 * TOK_MB))[None, :] + jitter
        chopped = jnp.sum((places[:, :, None] >= cuts[:, None, :]).astype(jnp.int32), axis=2)
    chosen = jax.random.randint(streams[5], (), 0, MICRO)
    rows = jnp.arange(MICRO, dtype=jnp.int32)[:, None] == chosen
    return jnp.where(rows, spanning, chopped).astype(jnp.int32)


def steps_of(own_key, extent, cuts, low, top_value):
    factor_of, own = 1.0, jax.random.fold_in(own_key, 6)
    for position, parts in cuts:
        draws = jnp.exp(jax.random.uniform(jax.random.fold_in(own, position), (parts,), jnp.float32, low / len(cuts), top_value / len(cuts)))
        factor_of = factor_of * jnp.repeat(draws, extent[position] // parts).reshape([-1 if axis == position else 1 for axis in range(len(extent))])
    return factor_of


def gaussian(own_key, shape, width, most, pieces=(), held_as=jnp.bfloat16):
    drawn = jax.random.normal(own_key, shape, jnp.float32) * width
    if len(pieces) > 0:
        drawn = steps_of(own_key, shape, pieces, -0.22, 0.18) * drawn
    return jnp.clip(drawn, min=-most, max=most).astype(held_as)


def setup_inputs(seed: int = 0) -> dict:
    splits = jax.random.split(jax.random.key(seed), 10)
    tokens = gaussian(splits[0], (MICRO, SEQ_LEN, D), 1.0, 6.0, ((1, 16),))
    w_qkv = gaussian(splits[1], (2, D, 3, D), D ** -0.5, 0.1875, ((0, 2), (3, 4)))
    w_out = gaussian(splits[2], (2, D, D), (D // 2) ** -0.5, 0.25, ((0, 2), (1, 4)))
    w_gate_up = gaussian(splits[3], (2, D, 2, FF), D ** -0.5, 0.1875, ((0, 2), (3, 4)))
    w_down = gaussian(splits[4], (2, FF, D), FF ** -0.5, 0.109375, ((0, 2), (1, 4)))
    norm_gains = jnp.clip(1.0 + 0.1 * jax.random.normal(splits[5], (2, 2, D), jnp.float32), 0.5, 1.5)
    log_decay = draw_log_decay(jax.random.fold_in(splits[9], 71), 0)
    segment_ids = draw_segment_ids(jax.random.fold_in(splits[9], 71), 0)
    cotangent = gaussian(splits[8], (MICRO, SEQ_LEN, D), 1.0, 6.0, ((1, 16),))
    return {"tokens": tokens, "w_qkv": w_qkv, "w_out": w_out, "w_gate_up": w_gate_up, "w_down": w_down, "norm_gains": norm_gains, "log_decay": log_decay, "segment_ids": segment_ids, "cotangent": cotangent}


epsilon = 1e-05
head_epsilon = 1.0
highest = lax.Precision.HIGHEST
far_below = -1e+30

@jax.custom_vjp
def low(v):
    return lax.optimization_barrier(v.astype(jnp.bfloat16)).astype(jnp.float32)

@jax.custom_vjp
def low_back(v):
    return v

def low_keep(v):
    return (low(v), None)

def low_pass(kept, grad):
    return (grad,)

def back_keep(v):
    return (v, None)

def back_low(kept, grad):
    return (low(grad),)
low.defvjp(low_keep, low_pass)
low_back.defvjp(back_keep, back_low)

def product(form, left, right):
    return jnp.einsum(form, left, right, precision=highest)

def rms_normed(values, gain_row):
    return values * lax.rsqrt(lax.optimization_barrier(jnp.mean(values * values, axis=-1, keepdims=True)) + epsilon) * gain_row

def causal_same(segments):
    length = segments.shape[-1]
    causal = jnp.arange(length)[:, None] >= jnp.arange(length)[None, :]
    return causal & (segments[..., :, None] == segments[..., None, :])

def diag_attention(query, keys, values, segments):
    length = query.shape[0]
    count = length // BLOCK
    query_b = query.reshape(count, BLOCK, HEADS, HDIM)
    keys_b = keys.reshape(count, BLOCK, HEADS, HDIM)
    values_b = values.reshape(count, BLOCK, HEADS, HDIM)
    allowed = causal_same(segments.reshape(count, BLOCK))
    scores = low_back(product('bqhd,bkhd->bhqk', query_b, keys_b)) * HDIM ** (-0.5)
    scores = jnp.where(allowed[:, None], scores, far_below)
    highest_score = lax.optimization_barrier(jnp.max(scores, axis=-1, keepdims=True))
    powers = jnp.exp(scores - highest_score)
    weights = low(powers / lax.optimization_barrier(jnp.sum(powers, axis=-1, keepdims=True)))
    attended = product('bhqk,bkhd->bqhd', weights, values_b)
    return low(low_back(attended)).reshape(length, HEADS * HDIM)

def norm_attention(query, keys, values, decays, segments):
    length = query.shape[0]
    count = length // BLOCK
    blocks = (query.reshape(count, BLOCK, HEADS, HDIM), keys.reshape(count, BLOCK, HEADS, HDIM), values.reshape(count, BLOCK, HEADS, HDIM), decays.reshape(count, BLOCK, HEADS), segments.reshape(count, BLOCK))

    def advance(carry, block):
        state, before = carry
        query_b, keys_b, values_b, decay_b, segment_b = block
        cumul = jnp.cumsum(decay_b, axis=0)
        allowed = causal_same(segment_b)[:, :, None]
        spread = cumul[:, None, :] - cumul[None, :, :]
        weight = jnp.where(allowed, jnp.exp(jnp.where(allowed, spread, 0.0)), 0.0)
        scored = low(low_back(product('qhd,khd->qkh', query_b, keys_b)) * weight)
        inner = product('qkh,khe->qhe', scored, values_b)
        reach = jnp.exp(cumul) * (segment_b == before)[:, None]
        outer = reach[:, :, None] * product('qhd,hde->qhe', query_b, state)
        final = segment_b[-1]
        kept = jnp.exp(cumul[-1][None, :] - cumul) * (segment_b == final)[:, None]
        carried = jnp.exp(cumul[-1]) * (before == final)
        state = carried[:, None, None] * state + product('khd,khe->hde', keys_b * kept[:, :, None], values_b)
        return ((state, final), inner + outer)
    start = (jnp.zeros((HEADS, HDIM, HDIM), jnp.float32), jnp.array(-1.0, jnp.float32))
    attended = lax.scan(jax.checkpoint(advance), start, blocks)[1]
    attended = low_back(attended.reshape(length, HEADS, HDIM))
    normed = attended * lax.rsqrt(lax.optimization_barrier(jnp.mean(attended * attended, axis=-1, keepdims=True)) + head_epsilon)
    return low(normed).reshape(length, HEADS * HDIM)

def layer(token_rows, first_kind, weights, decays, segments):
    w_qkv, w_out, w_gate_up, w_down, gain_pair = weights
    length = token_rows.shape[0]
    normed = low(rms_normed(token_rows, gain_pair[0]))
    projected = product('td,dcf->tcf', normed, w_qkv)
    query_raw = low_back(projected[:, 0]).reshape(length, HEADS, HDIM)
    keys_raw = low_back(projected[:, 1]).reshape(length, HEADS, HDIM)
    values_raw = low_back(projected[:, 2]).reshape(length, HEADS, HDIM)
    if first_kind:
        mixed = diag_attention(low(query_raw), low(keys_raw), low(values_raw), segments)
    else:
        mixed = norm_attention(low(jax.nn.silu(query_raw)), low(jax.nn.silu(keys_raw)), low(values_raw), decays, segments)
    middle = token_rows + low_back(jnp.dot(mixed, w_out, precision=highest))
    hidden_in = low(rms_normed(middle, gain_pair[1]))
    gate_up = product('td,dcf->tcf', hidden_in, w_gate_up)
    hidden = low(low_back(gate_up[:, 0]) * low_back(gate_up[:, 1]))
    return middle + low_back(jnp.dot(hidden, w_down, precision=highest))

def reference(tokens, w_qkv, w_out, w_gate_up, w_down, norm_gains, log_decay, segment_ids, cotangent):
    segments = segment_ids.astype(jnp.float32)

    def forward(inputs, bumps, qkv_all, out_all, gate_up_all, down_all, gains_all):
        firsts = []
        seconds = []
        for micro_index in range(MICRO):
            first_out = layer(inputs[micro_index], True, (qkv_all[0], out_all[0], gate_up_all[0], down_all[0], gains_all[0]), log_decay[micro_index], segments[micro_index])
            passed = low_back(low(first_out) + bumps[micro_index])
            second_out = layer(passed, False, (qkv_all[1], out_all[1], gate_up_all[1], down_all[1], gains_all[1]), log_decay[micro_index], segments[micro_index])
            firsts.append(first_out)
            seconds.append(second_out)
        return (jnp.stack(firsts), jnp.stack(seconds))
    inputs = tokens.astype(jnp.float32)
    outputs, pullback = jax.vjp(forward, inputs, jnp.zeros_like(inputs), w_qkv.astype(jnp.float32), w_out.astype(jnp.float32), w_gate_up.astype(jnp.float32), w_down.astype(jnp.float32), norm_gains.astype(jnp.float32))
    firsts, seconds = outputs
    grads = pullback((jnp.zeros_like(firsts), cotangent.astype(jnp.float32)))
    layer_outputs = jnp.stack([firsts, seconds]).astype(jnp.bfloat16)
    input_grads = jnp.stack([grads[0], grads[1]])
    return (layer_outputs, input_grads, grads[2], grads[3], grads[4], grads[5], grads[6])
```

```python
import functools

import jax
import jax.numpy as jnp
from jax import lax
from jax.experimental import pallas as pl
from jax.experimental.pallas import tpu as pltpu
from jax.sharding import PartitionSpec as P

HDIM = 64
BLOCK = 64
PAIR = 2 * HDIM
TILE = 256

epsilon = 1e-05
head_epsilon = 1.0
far_below = -1e30

F32 = jnp.float32
BF16 = jnp.bfloat16
vmem_limit = 56 * 1024 * 1024


def nn(a, b):
    return lax.dot_general(a, b, (((1,), (0,)), ((), ())), preferred_element_type=F32)


def nt(a, b):
    return lax.dot_general(a, b, (((1,), (1,)), ((), ())), preferred_element_type=F32)


def tn(a, b):
    return lax.dot_general(a, b, (((0,), (0,)), ((), ())), preferred_element_type=F32)


def tiles(extent):
    return [(at, min(TILE, extent - at)) for at in range(0, extent, TILE)]


def low_lanes(rows):
    return lax.broadcasted_iota(jnp.int32, (rows, PAIR), 1) < HDIM


def lane_masks(rows):
    low = low_lanes(rows)
    one = jnp.where(low, 1.0, 0.0)
    return low, one.astype(BF16), (1.0 - one).astype(BF16)


def stack2(pair, masks):
    return jnp.concatenate([pair * masks[1], pair * masks[2]], axis=0)


def pick(stacked, masks):
    rows = stacked.shape[0] // 2
    return jnp.where(masks[0], stacked[:rows], stacked[rows:])


def spread2(columns, at, masks):
    return jnp.where(masks[0], columns[:, at : at + 1], columns[:, at + 1 : at + 2])


def block_diagonal():
    rows = lax.broadcasted_iota(jnp.int32, (PAIR, PAIR), 0) < HDIM
    lanes = lax.broadcasted_iota(jnp.int32, (PAIR, PAIR), 1) < HDIM
    return rows == lanes


def by_rows(first, second):
    rows = lax.broadcasted_iota(jnp.int32, (PAIR, PAIR), 0) < HDIM
    return jnp.where(rows, first, second)


def pack_states(first, second):
    lanes = lax.broadcasted_iota(jnp.int32, (PAIR, PAIR), 1) < HDIM
    return jnp.where(
        lanes, first + pltpu.roll(first, HDIM, 1), second + pltpu.roll(second, HDIM, 1)
    )


def unpack_states(packed):
    lanes = lax.broadcasted_iota(jnp.int32, (PAIR, PAIR), 1) < HDIM
    turned = pltpu.roll(packed, HDIM, 1)
    mask = block_diagonal()
    return (
        jnp.where(mask, jnp.where(lanes, packed, turned), 0.0),
        jnp.where(mask, jnp.where(lanes, turned, packed), 0.0),
    )


def chain_sum(every, weights, which, heads):
    count = every.shape[0] // PAIR
    rows = lax.broadcasted_iota(jnp.int32, (PAIR, PAIR), 0) < HDIM
    lanes = lax.broadcasted_iota(jnp.int32, (PAIR, PAIR), 1) < HDIM

    def lap(at, total):
        base = (which * count + at) * heads
        weight = jnp.where(
            rows,
            jnp.where(lanes, weights[base], weights[base + 2]),
            jnp.where(lanes, weights[base + 1], weights[base + 3]),
        )
        start = pl.multiple_of(at * PAIR, PAIR)
        return total + weight * every[pl.ds(start, PAIR), :].astype(F32)

    return lax.fori_loop(0, count, lap, jnp.zeros((PAIR, PAIR), F32))


def stacked_position(rows):
    shape = (2 * rows, rows)
    at = lax.broadcasted_iota(jnp.int32, shape, 0)
    return (
        jnp.where(at >= rows, at - rows, at),
        lax.broadcasted_iota(jnp.int32, shape, 1),
        at < rows,
    )


def same_segment(columns, rows_meta, heads):
    seg = columns[:, heads : heads + 1]
    return jnp.concatenate([seg, seg], axis=0) == rows_meta[heads : heads + 1, :]


def load_start(flags, layer, sources, target, sem):
    own, own_far, own_near, other_far, other_near = sources
    half = target.shape[0] // 2
    mine, home, upper = (flags[0] == layer, flags[2] == 1, flags[1])
    far = target.at[pl.ds(pl.multiple_of(upper * half, half), half), :]
    near = target.at[pl.ds(pl.multiple_of((1 - upper) * half, half), half), :]

    @pl.when(mine & home)
    def _():
        pltpu.make_async_copy(own, target, sem).start()

    @pl.when(mine & jnp.logical_not(home))
    def _():
        pltpu.make_async_copy(own_far, far, sem).start()
        pltpu.make_async_copy(own_near, near, sem).start()

    @pl.when(jnp.logical_not(mine))
    def _():
        pltpu.make_async_copy(other_far, far, sem).start()
        pltpu.make_async_copy(other_near, near, sem).start()


def load_wait(sources, target, sem):
    pltpu.make_async_copy(sources[0], target, sem).wait()


def put_pieces(total, first, second, others):
    rows = first.shape[0]
    first[...] = total[:rows].astype(BF16)
    second[...] = total[rows : 2 * rows].astype(BF16)
    others[...] = total[2 * rows :].astype(BF16)


def joined(pieces):
    return jnp.concatenate([piece[...] for piece in pieces], axis=0)


def head_scale2(values, masks):
    squares = values * values
    first = jnp.sum(jnp.where(masks[0], squares, 0.0), axis=-1, keepdims=True)
    second = jnp.sum(jnp.where(masks[0], 0.0, squares), axis=-1, keepdims=True)
    return jnp.where(
        masks[0],
        lax.rsqrt(first / HDIM + head_epsilon),
        lax.rsqrt(second / HDIM + head_epsilon),
    )


def head_mean2(values, masks):
    first = jnp.sum(jnp.where(masks[0], values, 0.0), axis=-1, keepdims=True)
    second = jnp.sum(jnp.where(masks[0], 0.0, values), axis=-1, keepdims=True)
    return jnp.where(masks[0], first, second) / HDIM


def norm_kernel(x, gain, normed):
    values = x[...].astype(F32)
    scale = lax.rsqrt(jnp.mean(values * values, axis=-1, keepdims=True) + epsilon)
    normed[...] = (values * scale * gain[...]).astype(BF16)


def summed(own, across, far):
    rows = own.shape[0]
    return own[...].astype(F32) + across[:rows, :].astype(F32) + far[...].astype(F32)


def branch_kernel(x, own, across, far, gain, total, normed):
    values = x[...].astype(F32) + summed(own, across, far)
    kept = values.astype(total.dtype)
    total[...] = kept
    values = kept.astype(F32)
    scale = lax.rsqrt(jnp.mean(values * values, axis=-1, keepdims=True) + epsilon)
    normed[...] = (values * scale * gain[...]).astype(BF16)


def end_kernel(x, own, across, far, total):
    total[...] = (x[...].astype(F32) + summed(own, across, far)).astype(total.dtype)


def back_kernel(x, own, across, far, residual, gain, wide, narrow, grad_gain):
    values = x[...].astype(F32)
    grad_normed = summed(own, across, far)
    scale = lax.rsqrt(jnp.mean(values * values, axis=-1, keepdims=True) + epsilon)
    unit = values * scale
    grad_unit = grad_normed * gain[...]
    centre = jnp.mean(grad_unit * unit, axis=-1, keepdims=True)
    total = scale * (grad_unit - unit * centre) + residual[...].astype(F32)
    wide[...] = total
    narrow[...] = total.astype(BF16)
    grad_gain[...] = jnp.sum(grad_normed * unit, axis=0, keepdims=True)


def diag_probs(query, keys, masks, allowed):
    scores = nt(stack2(query, masks), keys) * HDIM ** (-0.5)
    scores = jnp.where(allowed, scores, far_below)
    powers = jnp.exp(scores - jnp.max(scores, axis=-1, keepdims=True))
    return powers * (1.0 / jnp.sum(powers, axis=-1, keepdims=True))


def diag_allowed(columns, rows_meta, heads, rows):
    at, before, _ = stacked_position(rows)
    near = (at >= before) & ((at // BLOCK) == (before // BLOCK))
    return near & same_segment(columns, rows_meta, heads)


def diag_forward_kernel(layer, heads, *refs):
    flags, a0, a1, a2, a3, columns, rows_meta = refs[:7]
    qkv_from, out_from = refs[7:12], refs[12:17]
    chosen, mixed, first, second, others, w_qkv, w_out, sems = refs[17:]
    load_start(flags, layer, qkv_from, w_qkv, sems.at[0])
    load_start(flags, layer, out_from, w_out, sems.at[1])
    x = joined((a0, a1, a2, a3))
    rows = a0.shape[0]
    width = heads * HDIM
    depth = x.shape[1]
    masks = lane_masks(rows)
    load_wait(qkv_from, w_qkv, sems.at[0])
    for part in range(3):
        product = nn(x, w_qkv[part * depth : (part + 1) * depth, :])
        chosen[:, part * width : (part + 1) * width] = product.astype(BF16)
    for piece in range(4):
        span = slice(piece * rows, (piece + 1) * rows)
        allowed = diag_allowed(columns[span, :], rows_meta[piece], heads, rows)
        for pair in range(heads // 2):
            q, k, v = (
                chosen[span, part * width + pair * PAIR : part * width + (pair + 1) * PAIR]
                for part in range(3)
            )
            weights = diag_probs(q, k, masks, allowed).astype(BF16)
            mixed[span, pair * PAIR : (pair + 1) * PAIR] = pick(nn(weights, v), masks).astype(BF16)
    load_wait(out_from, w_out, sems.at[1])
    put_pieces(nn(mixed[...], w_out[...]), first, second, others)


def diag_backward_kernel(layer, heads, *refs):
    flags, a0, a1, a2, a3, chosen, columns, rows_meta = refs[:8]
    qkv_from, out_from = refs[8:13], refs[13:18]
    grads, first, second, others, w_qkv, w_out, sems = refs[18:]
    load_start(flags, layer, out_from, w_out, sems.at[1])
    load_start(flags, layer, qkv_from, w_qkv, sems.at[0])
    g = joined((a0, a1, a2, a3))
    rows = a0.shape[0]
    width = heads * HDIM
    depth = g.shape[1]
    masks = lane_masks(rows)
    load_wait(out_from, w_out, sems.at[1])
    grad_mixed = nt(g, w_out[...]).astype(BF16)
    for piece in range(4):
        span = slice(piece * rows, (piece + 1) * rows)
        allowed = diag_allowed(columns[span, :], rows_meta[piece], heads, rows)
        for pair in range(heads // 2):
            q, k, v = (
                chosen[span, part * width + pair * PAIR : part * width + (pair + 1) * PAIR]
                for part in range(3)
            )
            grad = stack2(grad_mixed[span, pair * PAIR : (pair + 1) * PAIR], masks)
            probs = diag_probs(q, k, masks, allowed)
            grad_probs = nt(grad, v)
            centre = jnp.sum(grad_probs * probs, axis=-1, keepdims=True)
            grad_scores = (probs * (grad_probs - centre)).astype(BF16)
            grad_q = pick(nn(grad_scores, k), masks) * HDIM ** (-0.5)
            grad_k = tn(grad_scores, stack2(q, masks)) * HDIM ** (-0.5)
            grad_v = tn(probs.astype(BF16), grad)
            for part, member in enumerate((grad_q, grad_k, grad_v)):
                at = part * width + pair * PAIR
                grads[span, at : at + PAIR] = member.astype(BF16)
    load_wait(qkv_from, w_qkv, sems.at[0])
    put_back(grads, w_qkv, width, depth, first, second, others)


def put_back(grads, w_qkv, width, depth, first, second, others):
    total = nt(grads[:, :width], w_qkv[:depth, :])
    for part in range(1, 3):
        total = total + nt(
            grads[:, part * width : (part + 1) * width],
            w_qkv[part * depth : (part + 1) * depth, :],
        )
    put_pieces(total, first, second, others)


def norm_project_kernel(layer, heads, *refs):
    flags, coefs, a0, a1, a2, a3, columns = refs[:7]
    qkv_from = refs[7:12]
    chosen, slopes, states, ranges, w_qkv, sems = refs[12:]
    load_start(flags, layer, qkv_from, w_qkv, sems.at[0])
    x = joined((a0, a1, a2, a3))
    rows = a0.shape[0]
    width = heads * HDIM
    depth = x.shape[1]
    masks = lane_masks(rows)
    load_wait(qkv_from, w_qkv, sems.at[0])
    for part in range(3):
        product = nn(x, w_qkv[part * depth : (part + 1) * depth, :])
        if part < 2:
            sigmoid = 1.0 / (1.0 + jnp.exp(-product))
            slope = sigmoid * (1.0 + product * (1.0 - sigmoid))
            slopes[:, part * width : (part + 1) * width] = slope.astype(BF16)
            product = product * sigmoid
        chosen[:, part * width : (part + 1) * width] = product.astype(BF16)
    mask = block_diagonal()
    pairs = heads // 2
    for half in range(2):
        whole = []
        for pair in range(pairs):
            total = jnp.zeros((PAIR, PAIR), F32)
            for piece in (2 * half, 2 * half + 1):
                span = slice(piece * rows, (piece + 1) * rows)
                at = width + pair * PAIR
                k = chosen[span, at : at + PAIR].astype(F32)
                v = chosen[span, at + width : at + width + PAIR]
                kept = spread2(columns[span, :], heads + 1 + heads + 2 * pair, masks)
                state = jnp.where(mask, tn((k * kept).astype(BF16), v), 0.0)
                base = (piece * pairs + pair) * PAIR
                states[base : base + PAIR, :] = state.astype(BF16)
                u = (2 * 4 + piece) * heads + 2 * pair
                total = total + by_rows(coefs[u], coefs[u + 1]) * state
            whole.append(total)
        ranges[half * PAIR : (half + 1) * PAIR, :] = pack_states(*whole).astype(BF16)


def norm_weight(columns, rows_meta, heads, pair, rows):
    at, before, top = stacked_position(rows)
    first, second = 2 * pair, 2 * pair + 1
    cumul = jnp.concatenate(
        [columns[:, first : first + 1], columns[:, second : second + 1]], axis=0
    )
    other = jnp.where(top, rows_meta[first : first + 1, :], rows_meta[second : second + 1, :])
    allowed = (at >= before) & same_segment(columns, rows_meta, heads)
    return jnp.where(allowed, jnp.exp(jnp.minimum(cumul - other, 0.0)), 0.0)


def norm_inner_kernel(heads, chosen, columns, rows_meta, inner):
    rows = rows_meta.shape[2]
    width = heads * HDIM
    masks = lane_masks(rows)
    for piece in range(4):
        span = slice(piece * rows, (piece + 1) * rows)
        for pair in range(heads // 2):
            q, k, v = (
                chosen[span, part * width + pair * PAIR : part * width + (pair + 1) * PAIR]
                for part in range(3)
            )
            weight = norm_weight(columns[span, :], rows_meta[piece], heads, pair, rows)
            scored = (nt(stack2(q, masks), k) * weight).astype(BF16)
            inner[span, pair * PAIR : (pair + 1) * PAIR] = pick(nn(scored, v), masks)


def norm_outer_kernel(layer, heads, *refs):
    flags, coefs, weights, chosen, inner, states, every, columns = refs[:8]
    out_from = refs[8:13]
    raw, mixed, entering, first, second, others, w_out, sems = refs[13:]
    load_start(flags, layer, out_from, w_out, sems.at[0])
    rows = first.shape[0]
    width = heads * HDIM
    masks = lane_masks(rows)
    pairs = heads // 2
    prefixes = [unpack_states(chain_sum(every, weights, half, heads)) for half in range(2)]
    for piece in range(4):
        span = slice(piece * rows, (piece + 1) * rows)
        for pair in range(pairs):
            a = piece * heads + 2 * pair
            b = (4 + piece) * heads + 2 * pair
            base = ((piece ^ 1) * pairs + pair) * PAIR
            state = by_rows(coefs[a], coefs[a + 1]) * prefixes[piece // 2][pair]
            state = state + by_rows(coefs[b], coefs[b + 1]) * states[base : base + PAIR, :].astype(
                F32
            )
            state = state.astype(BF16)
            base = (piece * pairs + pair) * PAIR
            entering[base : base + PAIR, :] = state
            lanes = slice(pair * PAIR, (pair + 1) * PAIR)
            reach = spread2(columns[span, :], heads + 1 + 2 * pair, masks)
            out = inner[span, lanes] + reach * nn(chosen[span, lanes], state)
            raw[span, lanes] = out
            mixed[span, lanes] = (out * head_scale2(out, masks)).astype(BF16)
    load_wait(out_from, w_out, sems.at[0])
    put_pieces(nn(mixed[...], w_out[...]), first, second, others)


def norm_back_raw_kernel(layer, heads, *refs):
    flags, coefs, a0, a1, a2, a3, raw, chosen, columns = refs[:9]
    out_from = refs[9:14]
    grad_raw, grad_states, ranges, w_out, sems = refs[14:]
    load_start(flags, layer, out_from, w_out, sems.at[0])
    g = joined((a0, a1, a2, a3))
    rows = a0.shape[0]
    masks = lane_masks(rows)
    mask = block_diagonal()
    pairs = heads // 2
    load_wait(out_from, w_out, sems.at[0])
    grad_mixed = nt(g, w_out[...])
    for half in range(2):
        whole = []
        for pair in range(pairs):
            total = jnp.zeros((PAIR, PAIR), F32)
            lanes = slice(pair * PAIR, (pair + 1) * PAIR)
            for piece in (2 * half, 2 * half + 1):
                span = slice(piece * rows, (piece + 1) * rows)
                out = raw[span, lanes]
                scale = head_scale2(out, masks)
                unit = out * scale
                grad = grad_mixed[span, lanes]
                grad = (scale * (grad - unit * head_mean2(grad * unit, masks))).astype(BF16)
                grad_raw[span, lanes] = grad
                reach = spread2(columns[span, :], heads + 1 + 2 * pair, masks)
                q = (chosen[span, lanes].astype(F32) * reach).astype(BF16)
                state = jnp.where(mask, tn(q, grad), 0.0)
                base = (piece * pairs + pair) * PAIR
                grad_states[base : base + PAIR, :] = state.astype(BF16)
                a = piece * heads + 2 * pair
                total = total + by_rows(coefs[a], coefs[a + 1]) * state
            whole.append(total)
        ranges[half * PAIR : (half + 1) * PAIR, :] = pack_states(*whole).astype(BF16)


def norm_back_inner_kernel(heads, grad_raw, chosen, entering, columns, rows_meta, grads):
    rows = rows_meta.shape[2]
    width = heads * HDIM
    masks = lane_masks(rows)
    pairs = heads // 2
    for piece in range(4):
        span = slice(piece * rows, (piece + 1) * rows)
        for pair in range(pairs):
            lanes = slice(pair * PAIR, (pair + 1) * PAIR)
            q, k, v = (
                chosen[span, part * width + pair * PAIR : part * width + (pair + 1) * PAIR]
                for part in range(3)
            )
            weight = norm_weight(columns[span, :], rows_meta[piece], heads, pair, rows)
            queries = stack2(q, masks)
            scored = (nt(queries, k) * weight).astype(BF16)
            grad = grad_raw[span, lanes]
            stacked = stack2(grad, masks)
            grad_dots = (nt(stacked, v) * weight).astype(BF16)
            base = (piece * pairs + pair) * PAIR
            reach = spread2(columns[span, :], heads + 1 + 2 * pair, masks)
            grad_q = pick(nn(grad_dots, k), masks)
            grad_q = grad_q + reach * nt(grad, entering[base : base + PAIR, :])
            for part, member in enumerate((grad_q, tn(grad_dots, queries), tn(scored, stacked))):
                at = part * width + pair * PAIR
                grads[span, at : at + PAIR] = member


def norm_back_outer_kernel(layer, heads, *refs):
    flags, coefs, weights, partial, chosen, slopes, grad_states, every, columns = refs[:9]
    qkv_from = refs[9:14]
    grads, first, second, others, w_qkv, sems = refs[14:]
    load_start(flags, layer, qkv_from, w_qkv, sems.at[0])
    rows = first.shape[0]
    depth = first.shape[1]
    width = heads * HDIM
    masks = lane_masks(rows)
    pairs = heads // 2
    suffixes = [unpack_states(chain_sum(every, weights, half, heads)) for half in range(2)]
    for piece in range(4):
        span = slice(piece * rows, (piece + 1) * rows)
        for pair in range(pairs):
            b = (4 + (piece ^ 1)) * heads + 2 * pair
            u = (8 + piece) * heads + 2 * pair
            base = ((piece ^ 1) * pairs + pair) * PAIR
            state = by_rows(coefs[u], coefs[u + 1]) * suffixes[piece // 2][pair]
            state = state + by_rows(coefs[b], coefs[b + 1]) * grad_states[
                base : base + PAIR, :
            ].astype(F32)
            state = state.astype(BF16)
            at = pair * PAIR
            kept = spread2(columns[span, :], heads + 1 + heads + 2 * pair, masks)
            k = chosen[span, width + at : width + at + PAIR].astype(F32) * kept
            v = chosen[span, 2 * width + at : 2 * width + at + PAIR]
            grad_q = partial[span, at : at + PAIR]
            grad_k = partial[span, width + at : width + at + PAIR] + kept * nt(v, state)
            grad_v = partial[span, 2 * width + at : 2 * width + at + PAIR]
            grad_v = grad_v + nn(k.astype(BF16), state)
            grad_q = grad_q * slopes[span, at : at + PAIR].astype(F32)
            grad_k = grad_k * slopes[span, width + at : width + at + PAIR].astype(F32)
            grads[span, at : at + PAIR] = grad_q.astype(BF16)
            grads[span, width + at : width + at + PAIR] = grad_k.astype(BF16)
            grads[span, 2 * width + at : 2 * width + at + PAIR] = grad_v.astype(BF16)
    load_wait(qkv_from, w_qkv, sems.at[0])
    put_back(grads, w_qkv, width, depth, first, second, others)


def mixer_weights_kernel(heads, x0, x1, x2, x3, g0, g1, g2, g3, grads, mixed, out):
    x = joined((x0, x1, x2, x3))
    g = joined((g0, g1, g2, g3))
    depth = x.shape[1]
    width = heads * HDIM
    for part in range(3):
        product = tn(x, grads[:, part * width : (part + 1) * width])
        out[part * depth : (part + 1) * depth, :] = product.astype(BF16)
    out[3 * depth :, :] = tn(g, mixed[...]).astype(BF16)


def glu_forward_kernel(layer, *refs):
    flags, a0, a1, a2, a3 = refs[:5]
    gate_from, down_from = refs[5:10], refs[10:15]
    gates, ups, hiddens, first, second, others, w_gate, w_down, sems = refs[15:]
    load_start(flags, layer, gate_from, w_gate, sems.at[0])
    load_start(flags, layer, down_from, w_down, sems.at[1])
    x = joined((a0, a1, a2, a3))
    extent = gates.shape[1]
    load_wait(gate_from, w_gate, sems.at[0])
    for at, size in tiles(extent):
        gate = nt(x, w_gate[at : at + size, :])
        up = nt(x, w_gate[extent + at : extent + at + size, :])
        gates[:, at : at + size] = gate.astype(BF16)
        ups[:, at : at + size] = up.astype(BF16)
        hiddens[:, at : at + size] = (gate * up).astype(BF16)
    load_wait(down_from, w_down, sems.at[1])
    rows = a0.shape[0]
    for at, size in tiles(x.shape[1]):
        total = nn(hiddens[...], w_down[:, at : at + size])
        put_tile(total, rows, at, size, first, second, others)


def put_tile(total, rows, at, size, first, second, others):
    first[:, at : at + size] = total[:rows].astype(BF16)
    second[:, at : at + size] = total[rows : 2 * rows].astype(BF16)
    others[:, at : at + size] = total[2 * rows :].astype(BF16)


def glu_backward_kernel(layer, *refs):
    flags, a0, a1, a2, a3, gates, ups = refs[:7]
    gate_from, down_from = refs[7:12], refs[12:17]
    grad_gates, grad_ups, first, second, others, w_gate, w_down, sems = refs[17:]
    load_start(flags, layer, down_from, w_down, sems.at[1])
    load_start(flags, layer, gate_from, w_gate, sems.at[0])
    g = joined((a0, a1, a2, a3))
    extent = gates.shape[1]
    load_wait(down_from, w_down, sems.at[1])
    for at, size in tiles(extent):
        grad = nt(g, w_down[at : at + size, :])
        grad_gates[:, at : at + size] = (grad * ups[:, at : at + size].astype(F32)).astype(BF16)
        grad_ups[:, at : at + size] = (grad * gates[:, at : at + size].astype(F32)).astype(BF16)
    load_wait(gate_from, w_gate, sems.at[0])
    rows = a0.shape[0]
    for at, size in tiles(g.shape[1]):
        total = nn(grad_gates[...], w_gate[:extent, at : at + size])
        total = total + nn(grad_ups[...], w_gate[extent:, at : at + size])
        put_tile(total, rows, at, size, first, second, others)


def glu_weights_kernel(x0, x1, x2, x3, g0, g1, g2, g3, grad_gates, grad_ups, hiddens, out):
    x = joined((x0, x1, x2, x3))
    g = joined((g0, g1, g2, g3))
    extent = hiddens.shape[1]
    for at, size in tiles(extent):
        out[at : at + size, :] = tn(grad_gates[:, at : at + size], x).astype(BF16)
        out[extent + at : extent + at + size, :] = tn(grad_ups[:, at : at + size], x).astype(BF16)
        out[2 * extent + at : 2 * extent + at + size, :] = tn(
            hiddens[:, at : at + size], g
        ).astype(BF16)


VM = pl.BlockSpec(memory_space=pltpu.VMEM)
SM = pl.BlockSpec(memory_space=pltpu.SMEM)
ANY = pl.BlockSpec(memory_space=pl.ANY)


def call(kernel, name, operands, outs, scratch=(), flops=0):
    specs = [spec for spec, _ in operands]
    values = [value for _, value in operands]
    moved = sum(v.size * v.dtype.itemsize for v in values) + sum(
        jnp.dtype(kind).itemsize * functools.reduce(lambda a, b: a * b, shape) for shape, kind in outs
    )
    result = pl.pallas_call(
        kernel,
        name=name,
        out_shape=[jax.ShapeDtypeStruct(shape, kind) for shape, kind in outs],
        in_specs=specs,
        out_specs=[VM] * len(outs),
        scratch_shapes=list(scratch),
        compiler_params=pltpu.CompilerParams(vmem_limit_bytes=vmem_limit),
        cost_estimate=pl.CostEstimate(flops=flops, bytes_accessed=moved, transcendentals=0),
    )(*values)
    return result


def vm(*values):
    return [(VM, value) for value in values]


def sm(*values):
    return [(SM, value) for value in values]


def hbm(*values):
    return [(ANY, value) for value in values]


class Place:
    def __init__(self):
        self.seqs = lax.axis_size("seq")
        self.tensors = lax.axis_size("tensor")
        self.section = lax.axis_index("section")
        self.seq = lax.axis_index("seq")
        self.tensor = lax.axis_index("tensor")
        self.core = self.seq % 2
        self.upper = (self.seq // 2) % 2
        self.inner = self.tensor % 2
        self.outer = self.tensor // 2
        self.home = self.core == self.outer

    def pairs(self, chosen, move):
        return [
            (s * self.tensors + t, move(s, t)[0] * self.tensors + move(s, t)[1])
            for s in range(self.seqs)
            for t in range(self.tensors)
            if chosen(s % 2 == t // 2)
        ]

    def joint(self, value, chosen, move):
        return lax.ppermute(value, ("seq", "tensor"), self.pairs(chosen, move))

    def over_seq(self, value, bit):
        return lax.ppermute(value, "seq", [(s, s ^ bit) for s in range(self.seqs)])

    def over_tensor(self, value, bit):
        return lax.ppermute(value, "tensor", [(t, t ^ bit) for t in range(self.tensors)])

    def over_section(self, value):
        return lax.ppermute(value, "section", [(0, 1), (1, 0)])


def half_of(array, which):
    half = array.shape[0] // 2
    return lax.dynamic_slice_in_dim(array, which * half, half, 0)


def fetch(place, own):
    part = half_of(own, place.upper)
    own_far = place.joint(part, lambda home: home, lambda s, t: (s, t ^ 2))
    part = jnp.where(place.home, part, own_far)
    other_far = place.over_section(part)
    own_near = place.joint(part, lambda home: not home, lambda s, t: (s ^ 2, t))
    other_near = place.over_seq(other_far, 2)
    return (own, own_far, own_near, other_far, other_near)


def gather_rows(place, own):
    far = place.over_tensor(own, 1)
    across = place.over_seq(own, 1)
    both = place.over_seq(far, 1)
    return (own, far, across, both)


def scatter_rows(place, first, second, others):
    across = place.over_seq(others, 1)
    rows = first.shape[0]
    sent = (second.astype(F32) + across[rows:].astype(F32)).astype(BF16)
    return (first, across, place.over_tensor(sent, 1))


def gather_states(place, own):
    every = jnp.concatenate([own, place.over_tensor(own, 2)], axis=0)
    bit = 2
    while bit < place.seqs:
        every = jnp.concatenate([every, place.over_seq(every, bit)], axis=0)
        bit *= 2
    return every


def reduce_grads(place, grads, layer):
    sent = half_of(grads, 1 - place.upper)
    total = half_of(grads, place.upper)

    def add(a, b):
        return (a.astype(F32) + b.astype(F32)).astype(BF16)

    total = add(total, place.over_seq(sent, 2))
    bit = 4
    while bit < place.seqs:
        total = add(total, place.over_seq(total, bit))
        bit *= 2
    total = add(total, lax.ppermute(total, "section", [(1 - layer, layer)]))
    total = add(total, place.joint(total, lambda home: not home, lambda s, t: (s, t ^ 2)))
    near = place.joint(total, lambda home: home, lambda s, t: (s ^ 2, t))
    total = jnp.where(
        place.home, total, place.joint(total, lambda home: home, lambda s, t: (s ^ 1, t))
    )
    near = jnp.where(
        place.home, near, place.joint(near, lambda home: home, lambda s, t: (s ^ 1, t))
    )
    low = jnp.where(place.upper == 0, total, near)
    high = jnp.where(place.upper == 0, near, total)
    return jnp.concatenate([low, high], axis=0)


def member_ids(place):
    ids = [(0, 0), (0, 1)]
    bit = 2
    while bit < place.seqs:
        ids = ids + [(s | bit, k) for s, k in ids]
        bit *= 2
    return ids


def prepare(place, log_decay, segments, rows):
    heads = log_decay.shape[0]
    seqs, tensors = place.seqs, place.tensors
    shard = place.inner + 2 * place.core
    seg_all = lax.all_gather(segments, "seq", axis=0).reshape(seqs * tensors, rows)
    lasts = seg_all[:, -1]
    before = jnp.concatenate([jnp.full((1,), -1.0, F32), lasts[:-1]])
    decay_all = lax.all_gather(log_decay, ("seq", "tensor"), axis=0)
    decay_all = decay_all.reshape(seqs, tensors, heads, tensors, rows)
    decay_all = lax.dynamic_index_in_dim(decay_all, shard, 1, keepdims=False)
    decay_all = jnp.transpose(decay_all, (0, 2, 1, 3)).reshape(seqs * tensors, heads, rows)
    pair_seq = place.seq - place.core
    seqs_of = [place.seq, place.seq, place.seq ^ 1, place.seq ^ 1]
    tensors_of = [place.tensor, place.tensor ^ 1, place.tensor, place.tensor ^ 1]
    ids = [s * tensors + t for s, t in zip(seqs_of, tensors_of)]
    decay = jnp.stack(
        [lax.dynamic_index_in_dim(decay_all, at, 0, keepdims=False) for at in ids]
    )
    seg = jnp.stack([lax.dynamic_index_in_dim(seg_all, at, 0, keepdims=False) for at in ids])
    prior = jnp.stack([lax.dynamic_index_in_dim(before, at, 0, keepdims=False) for at in ids])
    upto = (jnp.arange(rows)[:, None] <= jnp.arange(rows)[None, :]).astype(F32)
    cumul = jnp.einsum("phu,ut->pht", decay, upto, precision=lax.Precision.HIGHEST)
    total = cumul[:, :, -1]
    last = seg[:, -1]
    reach = jnp.exp(cumul) * (seg == prior[:, None])[:, None]
    kept = jnp.exp(total[:, :, None] - cumul) * (seg == last[:, None])[:, None]
    rows_meta = jnp.concatenate([cumul, seg[:, None]], axis=1)
    columns = jnp.concatenate([cumul, seg[:, None], reach, kept], axis=1)
    columns = jnp.transpose(columns, (0, 2, 1)).reshape(4 * rows, 3 * heads + 1)
    order = jnp.array([0, 1, 0, 1]) ^ place.inner
    second = (order == 1)[:, None]
    partner = jnp.array([1, 0, 3, 2])
    carried = jnp.exp(total) * (prior == last)[:, None]
    a = jnp.where(second, carried[partner], 1.0)
    b = jnp.where(second, jnp.ones_like(a), 0.0)
    u = jnp.where(second, 1.0, carried[partner])
    coefs = jnp.stack([a, b, u]).reshape(-1)
    piece_totals = jnp.sum(decay_all, axis=-1)
    range_totals = jnp.sum(piece_totals.reshape(-1, 2, heads), axis=1)
    range_lasts = lasts[1::2]
    range_prior = before[::2]
    count = range_totals.shape[0]
    included = jnp.cumsum(range_totals, axis=0)
    excluded = included - range_totals
    apart = excluded[:, None] - included[None, :]
    linked = (jnp.arange(count)[:, None] > jnp.arange(count)[None, :]) & (
        range_prior[:, None] == range_lasts[None, :]
    )
    matrix = jnp.where(linked[..., None], jnp.exp(jnp.minimum(apart, 0.0)), 0.0)
    members = jnp.array(member_ids(place))
    member_seq = members[:, 0] ^ (place.seq - place.core)
    member_outer = members[:, 1] ^ place.outer
    cores = jnp.stack([place.core, 1 - place.core])
    every = ((member_seq[:, None] + cores[None, :]) * 2 + member_outer[:, None]).reshape(-1)
    mine = (place.seq - place.core + cores) * 2 + place.outer
    pick_every = (every[:, None] == jnp.arange(count)[None, :]).astype(F32)
    pick_mine = (mine[:, None] == jnp.arange(count)[None, :]).astype(F32)
    exact = lax.Precision.HIGHEST
    forward = jnp.einsum("ar,rsh,js->ajh", pick_mine, matrix, pick_every, precision=exact)
    backward = jnp.einsum("as,rsh,jr->ajh", pick_mine, matrix, pick_every, precision=exact)
    return columns, rows_meta, coefs, forward.reshape(-1), backward.reshape(-1)


def body(tokens, w_qkv, w_out, w_gate_up, w_down, norm_gains, log_decay, segment_ids, cotangent):
    place = Place()
    section = place.section
    rows, depth = tokens.shape[1:]
    heads = w_qkv.shape[-1] // HDIM
    width = heads * HDIM
    extent = w_gate_up.shape[-1]
    count = 4 * rows
    flags = jnp.stack([section, place.upper, place.home.astype(jnp.int32)]).astype(jnp.int32)

    def one_stream(array):
        return lax.dynamic_index_in_dim(array, section, 0, keepdims=False)

    x0 = one_stream(tokens)
    out_cotangent = one_stream(cotangent)
    gains_own = norm_gains[0]
    gains_other = place.over_section(gains_own)
    gains = [
        jnp.where(section == layer, gains_own, gains_other)[:, None, :] for layer in range(2)
    ]

    row_bf = ((rows, depth), BF16)
    row_f32 = ((rows, depth), F32)
    pieces = [row_bf, row_bf, ((2 * rows, depth), BF16)]
    dma = pltpu.SemaphoreType.DMA((2,))

    def normalise(x, gain):
        return call(norm_kernel, "normalise", vm(x, gain), [row_bf])[0]

    qkv_from = fetch(place, jnp.transpose(w_qkv[0], (1, 0, 2)).reshape(3 * depth, width))
    out_from = fetch(place, w_out[0])
    gate_from = fetch(
        place, jnp.transpose(w_gate_up[0], (1, 2, 0)).reshape(2 * extent, depth)
    )
    down_from = fetch(place, w_down[0])
    s_qkv = pltpu.VMEM((3 * depth, width), BF16)
    s_out = pltpu.VMEM((width, depth), BF16)
    s_gate = pltpu.VMEM((2 * extent, depth), BF16)
    s_down = pltpu.VMEM((extent, depth), BF16)

    columns, rows_meta, coefs, forward_weights, backward_weights = prepare(
        place,
        jnp.transpose(one_stream(log_decay), (1, 0)),
        one_stream(segment_ids).astype(F32),
        rows,
    )

    def branch(x, parts, gain, kind):
        return call(
            branch_kernel, "branch", vm(x, *parts, gain), [((rows, depth), kind), row_bf]
        )

    def glu_forward(layer, gathered):
        *kept, p0, p1, p2 = call(
            functools.partial(glu_forward_kernel, layer),
            "glu_forward",
            sm(flags) + vm(*gathered) + hbm(*gate_from, *down_from),
            [((count, extent), BF16)] * 3 + pieces,
            [s_gate, s_down, dma],
            6 * count * extent * depth,
        )
        return kept, scatter_rows(place, p0, p1, p2)

    def glu_backward(layer, gathered, kept):
        gates, ups, hiddens = kept
        grad_gates, grad_ups, p0, p1, p2 = call(
            functools.partial(glu_backward_kernel, layer),
            "glu_backward",
            sm(flags) + vm(*gathered, gates, ups) + hbm(*gate_from, *down_from),
            [((count, extent), BF16)] * 2 + pieces,
            [s_gate, s_down, dma],
            6 * count * extent * depth,
        )
        return (grad_gates, grad_ups, hiddens), scatter_rows(place, p0, p1, p2)

    def glu_weights(x, g, kept):
        return call(
            glu_weights_kernel,
            "glu_weights",
            vm(*x, *g, *kept),
            [((3 * extent, depth), BF16)],
            (),
            6 * count * extent * depth,
        )[0]

    def mixer_weights(x, g, grads, mixed):
        return call(
            functools.partial(mixer_weights_kernel, heads),
            "mixer_weights",
            vm(*x, *g, grads, mixed),
            [((4 * depth, width), BF16)],
            (),
            8 * count * width * depth,
        )[0]

    def back(x, parts, residual, gain):
        return call(
            back_kernel,
            "back",
            vm(x, *parts, residual, gain),
            [row_f32, row_bf, ((1, depth), F32)],
        )

    normed0 = gather_rows(place, normalise(x0, gains[0][0]))
    chosen0, mixed0, p0, p1, p2 = call(
        functools.partial(diag_forward_kernel, 0, heads),
        "diag_forward",
        sm(flags) + vm(*normed0, columns, rows_meta) + hbm(*qkv_from, *out_from),
        [((count, 3 * width), BF16), ((count, width), BF16)] + pieces,
        [s_qkv, s_out, dma],
        8 * count * width * depth,
    )
    middle0, hidden_in = branch(x0, scatter_rows(place, p0, p1, p2), gains[0][1], F32)
    hidden_in0 = gather_rows(place, hidden_in)
    kept0, parts = glu_forward(0, hidden_in0)
    x1, normed = branch(middle0, parts, gains[1][0], BF16)

    normed1 = gather_rows(place, normed)
    state_rows = 4 * (heads // 2) * PAIR
    chosen1, slopes, states, ranges = call(
        functools.partial(norm_project_kernel, 1, heads),
        "norm_project",
        sm(flags, coefs) + vm(*normed1, columns) + hbm(*qkv_from),
        [
            ((count, 3 * width), BF16),
            ((count, 2 * width), BF16),
            ((state_rows, PAIR), BF16),
            ((2 * PAIR, PAIR), BF16),
        ],
        [s_qkv, dma],
        6 * count * width * depth,
    )
    every = gather_states(place, ranges)
    (inner,) = call(
        functools.partial(norm_inner_kernel, heads),
        "norm_inner",
        vm(chosen1, columns, rows_meta),
        [((count, width), F32)],
        (),
        8 * count * width * rows,
    )
    raw, mixed1, entering, p0, p1, p2 = call(
        functools.partial(norm_outer_kernel, 1, heads),
        "norm_outer",
        sm(flags, coefs, forward_weights)
        + vm(chosen1, inner, states, every, columns)
        + hbm(*out_from),
        [((count, width), F32), ((count, width), BF16), ((state_rows, PAIR), BF16)] + pieces,
        [s_out, dma],
        2 * count * width * depth,
    )
    middle1, hidden_in = branch(x1, scatter_rows(place, p0, p1, p2), gains[1][1], F32)
    hidden_in1 = gather_rows(place, hidden_in)
    kept1, parts = glu_forward(1, hidden_in1)
    (y1,) = call(end_kernel, "layer_end", vm(middle1, *parts), [row_bf])

    grad_branch1 = gather_rows(place, out_cotangent)
    kept1, parts = glu_backward(1, grad_branch1, kept1)
    glu_grads1 = glu_weights(hidden_in1, grad_branch1, kept1)
    grad_middle, grad_narrow, gain_11 = back(middle1, parts, out_cotangent, gains[1][1])
    grad_attn1 = gather_rows(place, grad_narrow)
    grad_raw, grad_states, ranges = call(
        functools.partial(norm_back_raw_kernel, 1, heads),
        "norm_back_raw",
        sm(flags, coefs) + vm(*grad_attn1, raw, chosen1, columns) + hbm(*out_from),
        [((count, width), BF16), ((state_rows, PAIR), BF16), ((2 * PAIR, PAIR), BF16)],
        [s_out, dma],
        2 * count * width * depth,
    )
    every = gather_states(place, ranges)
    (partial,) = call(
        functools.partial(norm_back_inner_kernel, heads),
        "norm_back_inner",
        vm(grad_raw, chosen1, entering, columns, rows_meta),
        [((count, 3 * width), F32)],
        (),
        20 * count * width * rows,
    )
    grads1, p0, p1, p2 = call(
        functools.partial(norm_back_outer_kernel, 1, heads),
        "norm_back_outer",
        sm(flags, coefs, backward_weights)
        + vm(partial, chosen1, slopes, grad_states, every, columns)
        + hbm(*qkv_from),
        [((count, 3 * width), BF16)] + pieces,
        [s_qkv, dma],
        6 * count * width * depth,
    )
    parts = scatter_rows(place, p0, p1, p2)
    mixer_grads1 = mixer_weights(normed1, grad_attn1, grads1, mixed1)
    _, passed_grad, gain_10 = back(x1, parts, grad_middle, gains[1][0])

    grad_branch0 = gather_rows(place, passed_grad)
    kept0, parts = glu_backward(0, grad_branch0, kept0)
    glu_grads0 = glu_weights(hidden_in0, grad_branch0, kept0)
    grad_middle, grad_narrow, gain_01 = back(middle0, parts, passed_grad, gains[0][1])
    grad_attn0 = gather_rows(place, grad_narrow)
    grads0, p0, p1, p2 = call(
        functools.partial(diag_backward_kernel, 0, heads),
        "diag_backward",
        sm(flags) + vm(*grad_attn0, chosen0, columns, rows_meta) + hbm(*qkv_from, *out_from),
        [((count, 3 * width), BF16)] + pieces,
        [s_qkv, s_out, dma],
        8 * count * width * depth,
    )
    parts = scatter_rows(place, p0, p1, p2)
    mixer_grads0 = mixer_weights(normed0, grad_attn0, grads0, mixed0)
    first_grad, first_narrow, gain_00 = back(x0, parts, grad_middle, gains[0][0])

    glu_total = [reduce_grads(place, glu_grads0, 0), reduce_grads(place, glu_grads1, 1)]
    mixer_total = [reduce_grads(place, mixer_grads0, 0), reduce_grads(place, mixer_grads1, 1)]
    first = section == 0
    glu_total = jnp.where(first, *glu_total).astype(F32)
    mixer_total = jnp.where(first, *mixer_total).astype(F32)
    total_qkv = jnp.transpose(mixer_total[: 3 * depth].reshape(3, depth, width), (1, 0, 2))
    total_out = jnp.transpose(mixer_total[3 * depth :], (1, 0))
    total_gate_up = jnp.transpose(glu_total[: 2 * extent].reshape(2, extent, depth), (2, 0, 1))
    total_down = glu_total[2 * extent :]
    gains_all = jnp.concatenate([gain_00, gain_01, gain_10, gain_11], axis=0)
    gains_all = lax.psum(gains_all, ("section", "seq", "tensor"))
    total_gains = jnp.where(first, gains_all[:2], gains_all[2:])

    def both_streams(of_first, of_second, kind):
        kept = jnp.where(first, of_first, of_second)
        sent = jnp.where(first, of_second, of_first).astype(BF16)
        got = place.over_section(sent).astype(kind)
        kept = kept.astype(kind)
        return jnp.stack([jnp.where(first, kept, got), jnp.where(first, got, kept)])

    layer_outs = both_streams(x1, y1, BF16)
    input_grads = both_streams(first_grad, passed_grad.astype(F32), F32)
    return (
        layer_outs[None],
        input_grads[None],
        total_qkv[None],
        total_out[None],
        total_gate_up[None],
        total_down[None],
        total_gains[None],
    )


def solution(mesh):
    return jax.shard_map(
        body,
        mesh=mesh,
        in_specs=(
            P(None, ("seq", "tensor"), None),
            P("section", None, None, "tensor"),
            P("section", "tensor", None),
            P("section", None, None, "tensor"),
            P("section", "tensor", None),
            P("section", None, None),
            P(None, "seq", "tensor"),
            P(None, "seq"),
            P(None, ("seq", "tensor"), None),
        ),
        out_specs=(
            P("section", None, ("seq", "tensor"), None),
            P("section", None, ("seq", "tensor"), None),
            P("section", None, None, "tensor"),
            P("section", "tensor", None),
            P("section", None, None, "tensor"),
            P("section", "tensor", None),
            P("section", None, None),
        ),
        check_vma=False,
    )
```
